512 devices in a mesh: row: 32 (over y, x), col: 16 (over z, core).
Axes of the slice: x: 4, y: 8, z: 8, core: 2. Of those that a mesh axis runs over, the one named last changes fastest.
Arguments:
- inputs: int32 [8, 128, 128], replicated, may hold values 0 or 1
- targets: int32 [8, 128, 128], replicated, may hold values 0 or 1
- initial_spikes: int32 [128, 128, 128], P(None, 'row'), may hold values 0 or 1
- w_in: bfloat16 [128, 128, 128], P(None, 'row'), may hold values from -0.5 to 0.5
- w_rec: bfloat16 [128, 128, 128, 128], P(None, 'col', 'row'), may hold values from -0.046875 to 0.046875
- w_out: bfloat16 [128, 128, 128], P('row'), may hold values from -0.046875 to 0.046875
- feedback: bfloat16 [128, 128, 128], P(None, 'row')
- adapt_gain: float32 [128, 128], P('row'), may hold values from 0.1 to 2
- adapt_decay: float32 [128, 128], P('row'), may hold values from 0.8 to 0.99
Outputs:
- readout: float32 [8, 128, 128], replicated
- grad_clipped: float32 [128, 128, 128, 128], P(None, 'col', 'row')
The draws below stay inside these ranges and needn't reach their ends.
All inputs are finite; a program needn't handle non-finite values. No bound on the sum of `initial_spikes` on one device may be relied on, other than what follows from the above.
Results may differ from the reference program's by a relative error of at most 0.0015.
Values may be sent and summed in bfloat16 or wider, within the bound.
A program may use at most 128 MiB of HBM per device.

```python
import math
import jax
import jax.numpy as jnp
from jax import lax

NA = 128
NB = 128
NIN = 128
K = 128
T_SIZE = 8
B = 128


def draw_feedback(key, part):
    position = jnp.arange(NA, dtype=jnp.float32) / max(NA - 1, 1)
    ramp = 1.0 + 2.0 * position
    base = jax.random.normal(key, (K, NA, NB), jnp.float32)
    ramp = ramp / jnp.sqrt(jnp.mean(ramp * ramp))
    values = base * ramp[None, :, None] * K ** (-0.5)
    return values.astype(jnp.bfloat16)


def plant(drawn, own_key, low, top_value):
    place = [jax.random.randint(jax.random.fold_in(own_key, axis), (), 0, length) for axis, length in enumerate(drawn.shape)]
    widest = drawn.shape.index(max(drawn.shape))
    next_to = place[:widest] + [(place[widest] + 1) % drawn.shape[widest]] + place[widest + 1:]
    return drawn.at[tuple(place)].set(low).at[tuple(next_to)].set(top_value)


def steps_of(key, extent, split, least, largest):
    level, own = 1.0, jax.random.fold_in(key, 6)
    for dim, shards_of in split:
        steps = jnp.exp(jax.random.uniform(jax.random.fold_in(own, dim), (shards_of,), jnp.float32, least / len(split), largest / len(split)))
        level = level * jnp.repeat(steps, extent[dim] // shards_of).reshape([-1 if axis == dim else 1 for axis in range(len(extent))])
    return level


def centred(key, shape, deviation, limit, shards=(), kind=jnp.bfloat16):
    gain = steps_of(key, shape, shards, -0.22, 0.18) if shards else 1.0
    values = jax.random.normal(key, shape, jnp.float32) * deviation * gain
    return jnp.minimum(jnp.maximum(values, -limit), limit).astype(kind)


def setup_inputs(seed: int = 0) -> dict:
    arg_keys = jax.random.split(jax.random.key(seed), 10)
    inputs = plant((jax.random.randint(arg_keys[0], (T_SIZE, B, NIN), 0, 5) < 1).astype(jnp.int32), jax.random.fold_in(arg_keys[0], 1), 0, 1)
    targets = plant((jax.random.randint(arg_keys[1], (T_SIZE, B, K), 0, 4) < 1).astype(jnp.int32), jax.random.fold_in(arg_keys[1], 1), 0, 1)
    initial_spikes = plant((jax.random.randint(arg_keys[2], (B, NA, NB), 0, 2) < 1).astype(jnp.int32), jax.random.fold_in(arg_keys[2], 1), 0, 1)
    w_in = centred(arg_keys[3], (NIN, NA, NB), NIN ** -0.5, 0.5, ((1, 32),))
    w_rec = centred(arg_keys[4], (NA, NB, NA, NB), (NA * NB) ** -0.5, 0.046875, ((1, 16), (2, 32)))
    w_out = centred(arg_keys[5], (NA, NB, K), (NA * NB) ** -0.5, 0.046875, ((0, 32),))
    feedback = draw_feedback(jax.random.fold_in(arg_keys[9], 71), 0)
    adapt_gain = jnp.clip(jnp.exp(math.log(2.0) - 2.9957323 * jax.random.uniform(arg_keys[7], (NA, NB), jnp.float32) ** steps_of(arg_keys[7], (NA, NB), ((0, 32),), -0.2, 0.2)), 0.1, 2.0)
    adapt_decay = jnp.clip(0.8 + 0.19 * jax.random.uniform(arg_keys[8], (NA, NB), jnp.float32) ** steps_of(arg_keys[8], (NA, NB), ((0, 32),), -0.2, 0.2), 0.8, 0.99)
    return {"inputs": inputs, "targets": targets, "initial_spikes": initial_spikes, "w_in": w_in, "w_rec": w_rec, "w_out": w_out, "feedback": feedback, "adapt_gain": adapt_gain, "adapt_decay": adapt_decay}


cellular_leak_multiplier = 0.8
readout_decay = 0.8

def reference(inputs, targets, initial_spikes, w_in, w_rec, w_out, feedback, adapt_gain, adapt_decay):
    neurons = NA * NB
    rows_all = T_SIZE * B
    external = jnp.dot(inputs.reshape(rows_all, NIN).astype(jnp.bfloat16), w_in.reshape(NIN, neurons), preferred_element_type=jnp.float32).reshape(T_SIZE, B, neurons)
    weights = w_rec.reshape(neurons, neurons)
    coupling_magnitude = adapt_gain.reshape(neurons)
    retention = adapt_decay.reshape(neurons)

    def advance(state, drive_now):
        pulse_output, cellular_charge, barrier_shift_amount, sender_trace = state
        spike_float = pulse_output.astype(jnp.float32)
        sender_trace = cellular_leak_multiplier * sender_trace + spike_float
        current = drive_now + jnp.dot(pulse_output, weights, preferred_element_type=jnp.float32)
        cellular_charge = cellular_leak_multiplier * cellular_charge + current - spike_float
        barrier_shift_amount = retention * barrier_shift_amount + spike_float
        present_emission_frequency = jax.nn.sigmoid(cellular_charge - 1.0 - coupling_magnitude * barrier_shift_amount)
        surrogate_slope = present_emission_frequency * (1.0 - present_emission_frequency)
        pulse_output = present_emission_frequency.astype(jnp.bfloat16)
        return ((pulse_output, cellular_charge, barrier_shift_amount, sender_trace), (sender_trace.astype(jnp.bfloat16), surrogate_slope, pulse_output))
    zeros = jnp.zeros((B, neurons), jnp.float32)
    start_state = (initial_spikes.reshape(B, neurons).astype(jnp.bfloat16), zeros, zeros, zeros)
    _, (traces, slopes, spikes) = lax.scan(advance, start_state, external)
    projected = jnp.dot(spikes.reshape(rows_all, neurons), w_out.reshape(neurons, K), preferred_element_type=jnp.float32).reshape(T_SIZE, B, K)

    def smooth(level, incoming):
        level = readout_decay * level + incoming
        return (level, level)
    _, readout = lax.scan(smooth, jnp.zeros((B, K), jnp.float32), projected)
    errors = (jax.nn.sigmoid(readout) - targets.astype(jnp.float32)).reshape(rows_all, K)
    err_high = errors.astype(jnp.bfloat16)
    err_low = (errors - err_high.astype(jnp.float32)).astype(jnp.bfloat16)
    fb_flat = feedback.reshape(K, neurons)
    signal = jnp.dot(err_high, fb_flat, preferred_element_type=jnp.float32) + jnp.dot(err_low, fb_flat, preferred_element_type=jnp.float32)
    signal = signal.reshape(T_SIZE, B, neurons)
    weighted = signal * slopes
    decays = retention - slopes * coupling_magnitude

    def backward(carried, inputs_now):
        weighted_now, decay_now = inputs_now
        return (weighted_now + decay_now * carried, carried)
    _, future = lax.scan(backward, zeros, (weighted, decays), reverse=True)
    factors = (weighted - coupling_magnitude * slopes * future).astype(jnp.bfloat16)
    grad = lax.dot_general(traces.reshape(rows_all, neurons), factors.reshape(rows_all, neurons), (((0,), (0,)), ((), ())), preferred_element_type=jnp.float32)
    squares = jnp.sum(grad * grad)
    clip_factor = jnp.minimum(1.0, NA * NB / 16.0 / jnp.sqrt(squares + 1e-06))
    return (readout, (grad * clip_factor).reshape(NA, NB, NA, NB))
```

```python
import functools

import jax
import jax.numpy as jnp
from jax import lax
from jax.experimental import pallas as pl
from jax.experimental.pallas import tpu as pltpu
from jax.sharding import PartitionSpec as P

MESH = pl.DeviceIdType.MESH
LEAK = 0.8
READ_DECAY = 0.8
F32 = jnp.float32
BF16 = jnp.bfloat16


def outward(i, n):
    return n // 2 + (1 - 2 * (i % 2)) * ((i + 1) // 2)


def kernel(dims, wt, fbt, gain, decay, s0, wint, inp, tgt, wo, grad, readout, clip,
           S, F, CS, CR, CT, ext, v, u, PS, PR, QS, QR, RO, rd, TR, tr, SL, WG, FT, sq, N1, N2,
           s_sem, f_sem, c_sem, p_sem, q_sem, r_sem, n_sem):
    ny, nx, nz, nk, nb, steps, neurons = dims
    rows, cols = ny * nx, nz * nk
    r, c = lax.axis_index("row"), lax.axis_index("col")
    y, x, z, k = r // nx, r % nx, c // nk, c % nk
    own = s0.shape[0]
    batch = s0.shape[1]
    ns, nr = wt.shape[1], wt.shape[0]
    kn = tgt.shape[1]
    kp = kn // cols
    groups = nr // nb

    def row_peer(j):
        return ((y + outward(j // nx, ny)) % ny) * nx + (x + outward(j % nx, nx)) % nx

    def col_peer(j):
        return ((z + outward(j // nk, nz)) % nz) * nk + (k + outward(j % nk, nk)) % nk

    def to_rows(fn, sem):
        def one(j, _):
            p = row_peer(j)
            src, dst = fn(p)
            pltpu.make_async_remote_copy(src_ref=src, dst_ref=dst, send_sem=sem.at[0], recv_sem=sem.at[1],
                                         device_id=(p, c), device_id_type=MESH).start()
            return 0
        lax.fori_loop(0, rows - 1, one, 0)

    def to_cols(fn, sem):
        def one(j, _):
            p = col_peer(j)
            src, dst = fn(p)
            pltpu.make_async_remote_copy(src_ref=src, dst_ref=dst, send_sem=sem.at[0], recv_sem=sem.at[1],
                                         device_id=(r, p), device_id_type=MESH).start()
            return 0
        lax.fori_loop(0, cols - 1, one, 0)

    def settle(ref, sem):
        pltpu.make_async_copy(ref, ref, sem).wait()

    barrier = pltpu.get_barrier_semaphore()

    def greet_row(j, _):
        pl.semaphore_signal(barrier, inc=1, device_id=(row_peer(j), c), device_id_type=MESH)
        return 0

    def greet_col(j, _):
        pl.semaphore_signal(barrier, inc=1, device_id=(r, col_peer(j)), device_id_type=MESH)
        return 0

    lax.fori_loop(0, rows - 1, greet_row, 0)
    lax.fori_loop(0, cols - 1, greet_col, 0)

    own_rows = pl.ds(pl.multiple_of(r * own, own), own)
    own_k = pl.ds(pl.multiple_of(c * kp, kp), kp)

    def piece(ref):
        return jnp.concatenate([ref[pl.ds(pl.multiple_of(a * nb + c * 8, 8), 8), :] for a in range(groups)], axis=0)

    g_own, d_own = piece(gain), piece(decay)
    for t in range(steps):
        ext[t] = lax.dot_general(wint[...], inp[t], (((1,), (1,)), ((), ())), preferred_element_type=F32)
    v[...] = jnp.zeros_like(v)
    u[...] = jnp.zeros_like(u)
    tr[...] = jnp.zeros_like(tr)
    rd[...] = jnp.zeros_like(rd)
    S[0, own_rows, :] = s0[...]
    pl.semaphore_wait(barrier, rows + cols - 2)
    to_rows(lambda p: (S.at[0, own_rows], S.at[0, own_rows]), s_sem.at[0])

    def sum_cols(t):
        settle(PR.at[t, pl.ds(0, cols - 1)], p_sem.at[t, 1])
        QS[t] = jnp.sum(PR[t], axis=0)
        QR[t, r] = QS[t]
        to_rows(lambda p: (QS.at[t], QR.at[t, r]), q_sem.at[t])

    def sum_rows(t):
        settle(QR.at[t, pl.ds(0, rows - 1)], q_sem.at[t, 1])
        RO[t, own_k, :] = jnp.sum(QR[t], axis=0)
        to_cols(lambda p: (RO.at[t, own_k], RO.at[t, own_k]), r_sem.at[t])

    def slope(t):
        settle(F.at[t, pl.ds(0, cols - 1)], f_sem.at[t, 1])
        for cc in range(cols):
            f = F[t, cc].astype(F32)
            sl = f * (1.0 - f)
            for a in range(groups):
                SL[t, a * nb + cc * 8:a * nb + cc * 8 + 8, :] = sl[a * 8:a * 8 + 8]

    def learn(t):
        settle(RO.at[t, pl.ds(0, (cols - 1) * kp)], r_sem.at[t, 1])
        level = READ_DECAY * rd[...] + RO[t]
        rd[...] = level
        readout[t] = level.T
        err = jax.nn.sigmoid(level) - tgt[t]
        high = err.astype(BF16)
        low = (err - high.astype(F32)).astype(BF16)
        signal = jnp.dot(fbt[...], high, preferred_element_type=F32) + jnp.dot(fbt[...], low, preferred_element_type=F32)
        WG[t] = signal * SL[t]

    def step(t, _):
        settle(S.at[t, pl.ds(0, (rows - 1) * own)], s_sem.at[t, 1])
        ct = jnp.dot(wt[...], S[t], preferred_element_type=F32)
        CT[...] = ct
        for cc in range(cols):
            CS[t, cc] = jnp.concatenate(
                [ct[a * nb + cc * 8:a * nb + cc * 8 + 8] for a in range(groups)], axis=0).astype(BF16)
        to_cols(lambda p: (CS.at[t, p], CR.at[t, c]), c_sem.at[t])
        CR[t, c] = jnp.zeros((own, batch), BF16)

        @pl.when(t >= 1)
        def _():
            sum_cols(t - 1)
            slope(t - 1)

        @pl.when(t >= 2)
        def _():
            sum_rows(t - 2)

        now = LEAK * tr[...] + S[t].astype(F32)
        tr[...] = now
        TR[t] = now.astype(BF16)

        @pl.when(t >= 3)
        def _():
            learn(t - 3)

        settle(CR.at[t, pl.ds(0, cols - 1)], c_sem.at[t, 1])
        current = ext[t] + piece(CT) + jnp.sum(CR[t].astype(F32), axis=0)
        spike = S[t, own_rows, :].astype(F32)
        volt = LEAK * v[...] + current - spike
        adapt = d_own * u[...] + spike
        v[...] = volt
        u[...] = adapt
        rate = jax.nn.sigmoid(volt - 1.0 - g_own * adapt).astype(BF16)
        F[t, c] = rate

        @pl.when(t + 1 < steps)
        def _():
            S[t + 1, own_rows, :] = rate
            to_rows(lambda p: (S.at[t + 1, own_rows], S.at[t + 1, own_rows]), s_sem.at[t + 1])

        PS[t] = lax.dot_general(wo[...], rate, (((0,), (0,)), ((), ())), preferred_element_type=F32)
        to_cols(lambda p: (PS.at[t, pl.ds(pl.multiple_of(p * kp, kp), kp)], PR.at[t, c]), p_sem.at[t])
        PR[t, c] = PS[t, own_k, :]
        to_cols(lambda p: (F.at[t, c], F.at[t, c]), f_sem.at[t])
        return 0

    lax.fori_loop(0, steps, step, 0)
    last = steps - 1
    sum_cols(last)
    sum_rows(last - 1)
    slope(last)
    learn(last - 2)
    sum_rows(last)
    learn(last - 1)
    learn(last)

    chunk = min(64, nr)

    def back(i, _):
        at = pl.ds(pl.multiple_of(i * chunk, chunk), chunk)
        g, d = gain[at, :], decay[at, :]
        future = jnp.zeros((chunk, batch), F32)
        for t in reversed(range(steps)):
            w, sl = WG[t, at, :], SL[t, at, :]
            gs = g * sl
            FT[t, at, :] = (w - gs * future).astype(BF16)
            future = w + (d - gs) * future
        return 0

    lax.fori_loop(0, nr // chunk, back, 0)

    block = min(256, ns)
    sq[...] = jnp.zeros_like(sq)

    def grads(i, _):
        at = pl.ds(pl.multiple_of(i * block, block), block)
        lhs = jnp.concatenate([TR[t, at, :] for t in range(steps)], axis=1)
        rhs = jnp.concatenate([FT[t] for t in range(steps)], axis=1)
        out = lax.dot_general(lhs, rhs, (((1,), (1,)), ((), ())), preferred_element_type=F32)
        grad[at, :] = out
        two = jnp.sum((out * out).reshape(block // 8, 8, nr), axis=0)
        sq[...] += sum(two[:, i * 128:(i + 1) * 128] for i in range(nr // 128))
        return 0

    lax.fori_loop(0, ns // block, grads, 0)
    N1[r] = sq[...]
    to_rows(lambda p: (sq, N1.at[r]), n_sem.at[0])
    settle(N1.at[pl.ds(0, rows - 1)], n_sem.at[0, 1])
    settle(N1.at[pl.ds(0, rows - 1)], n_sem.at[0, 0])
    sq[...] = jnp.sum(N1[...], axis=0)
    N2[c] = sq[...]
    to_cols(lambda p: (sq, N2.at[c]), n_sem.at[1])
    settle(N2.at[pl.ds(0, cols - 1)], n_sem.at[1, 1])
    total = jnp.sum(jnp.sum(N2[...], axis=0), keepdims=True)
    factor = jnp.minimum(1.0, neurons / 16.0 / jnp.sqrt(total + 1e-06))
    clip[...] = jnp.broadcast_to(factor, clip.shape)

    def ends(t, _):
        settle(S.at[t, pl.ds(0, (rows - 1) * own)], s_sem.at[t, 0])
        settle(F.at[t, pl.ds(0, cols - 1)], f_sem.at[t, 0])
        settle(CR.at[t, pl.ds(0, cols - 1)], c_sem.at[t, 0])
        settle(PR.at[t, pl.ds(0, cols - 1)], p_sem.at[t, 0])
        settle(QR.at[t, pl.ds(0, rows - 1)], q_sem.at[t, 0])
        settle(RO.at[t, pl.ds(0, (cols - 1) * kp)], r_sem.at[t, 0])
        return 0

    lax.fori_loop(0, steps, ends, 0)
    settle(N2.at[pl.ds(0, cols - 1)], n_sem.at[1, 0])


def body(dims, inputs, targets, initial_spikes, w_in, w_rec, w_out, feedback, adapt_gain, adapt_decay):
    ny, nx, nz, nk, nb, steps, neurons = dims
    rows, cols = ny * nx, nz * nk
    batch, channels = inputs.shape[1:]
    own_cols, groups = w_rec.shape[1], w_rec.shape[2]
    own = groups * own_cols
    ns, nr = w_rec.shape[0] * own_cols, groups * nb
    kn = w_out.shape[2]
    kp = kn // cols
    start = lax.axis_index("col") * own_cols

    def part(array, dim):
        return lax.dynamic_slice_in_dim(array, start, own_cols, dim)

    wt = w_rec.reshape(ns, nr).T
    fbt = feedback.reshape(kn, nr).T
    gain = jnp.broadcast_to(adapt_gain.reshape(nr, 1), (nr, batch))
    decay = jnp.broadcast_to(adapt_decay.reshape(nr, 1), (nr, batch))
    s0 = part(initial_spikes, 2).reshape(batch, own).T.astype(BF16)
    wint = part(w_in, 2).reshape(channels, own).T
    inp = inputs.astype(BF16)
    tgt = targets.astype(F32).swapaxes(1, 2)
    wo = part(w_out, 1).reshape(own, kn)
    dma = pltpu.SemaphoreType.DMA
    V = pltpu.VMEM
    vm = pl.BlockSpec(memory_space=pltpu.VMEM)
    grad, readout, clip = pl.pallas_call(
        functools.partial(kernel, dims),
        out_shape=(
            jax.ShapeDtypeStruct((ns, nr), F32),
            jax.ShapeDtypeStruct((steps, batch, kn), F32),
            jax.ShapeDtypeStruct((8, 128), F32),
        ),
        in_specs=[vm] * 9,
        out_specs=(vm, vm, vm),
        scratch_shapes=[
            V((steps, ns, batch), BF16),
            V((steps, cols, own, batch), BF16),
            V((steps, cols, own, batch), BF16),
            V((steps, cols, own, batch), BF16),
            V((nr, batch), F32),
            V((steps, own, batch), F32),
            V((own, batch), F32),
            V((own, batch), F32),
            V((steps, kn, batch), F32),
            V((steps, cols, kp, batch), F32),
            V((steps, kp, batch), F32),
            V((steps, rows, kp, batch), F32),
            V((steps, kn, batch), F32),
            V((kn, batch), F32),
            V((steps, ns, batch), BF16),
            V((ns, batch), F32),
            V((steps, nr, batch), F32),
            V((steps, nr, batch), F32),
            V((steps, nr, batch), BF16),
            V((8, 128), F32),
            V((rows, 8, 128), F32),
            V((cols, 8, 128), F32),
            dma((steps, 2)), dma((steps, 2)), dma((steps, 2)), dma((steps, 2)), dma((steps, 2)), dma((steps, 2)),
            dma((2, 2)),
        ],
        compiler_params=pltpu.CompilerParams(
            collective_id=0, has_side_effects=True, vmem_limit_bytes=48 * 2**20
        ),
    )(wt, fbt, gain, decay, s0, wint, inp, tgt, wo)
    return readout, (grad * clip[0, 0]).reshape(w_rec.shape)


def build(mesh, split, na, nb, steps):
    dims = (*split, nb, steps, na * nb)
    placed = (
        P(),
        P(),
        P(None, "row", None),
        P(None, "row", None),
        P(None, "col", "row", None),
        P("row", None, None),
        P(None, "row", None),
        P("row", None),
        P("row", None),
    )
    return jax.shard_map(
        functools.partial(body, dims), mesh=mesh, in_specs=placed,
        out_specs=(P(), P(None, "col", "row", None)), check_vma=False,
    )


def solution(mesh):
    return build(mesh, (8, 4, 8, 2), 128, 128, 8)
```

```python
import functools

import jax
import jax.numpy as jnp
from jax import lax
from jax.experimental import pallas as pl
from jax.experimental.pallas import tpu as pltpu
from jax.sharding import PartitionSpec as P

MESH = pl.DeviceIdType.MESH
LEAK = 0.8
READ_DECAY = 0.8
F32 = jnp.float32
BF16 = jnp.bfloat16


def rem(a, b):
    return a % b if isinstance(a, int) else lax.rem(a, jnp.int32(b))


def div(a, b):
    return a // b if isinstance(a, int) else lax.div(a, jnp.int32(b))


def outward(i, n):
    return n // 2 + (1 - 2 * rem(i, 2)) * div(i + 1, 2)


def kernel(dims, w_hbm, inp_hbm, tgt_hbm, s0_hbm, win_hbm, wo_hbm, fb_hbm, gain_hbm, decay_hbm, grad_hbm, levels_hbm, clip_hbm,
           grad, levels, clip,
           wb, wf, wt, inp, tgt, s0, small, wob, smallf, gain_ref, decay_ref, nat, fbt, winb, wok, gain, decay, ext,
           S, SR, F, CS, CR, CT, v, u, QS, QR, RO, rd, TR, tr, SL, WG, FT, sq, N1, N2,
           in_sem, s_sem, f_sem, c_sem, q_sem, r_sem, n_sem, out_sem):
    ny, nx, nz, nk, nb, steps, neurons = dims
    rows, cols = ny * nx, nz * nk
    r, c = lax.axis_index("row"), lax.axis_index("col")
    y, x, z, k = div(r, nx), rem(r, nx), div(c, nk), rem(c, nk)
    batch = inp.shape[1]
    half = batch // 2
    nr, ns = wt.shape
    kn = tgt.shape[2]
    kp = kn // cols
    groups = nr // nb
    own = groups * 8 // 2

    def row_peer(j):
        return rem(y + outward(div(j, nx), ny), ny) * nx + rem(x + outward(rem(j, nx), nx), nx)

    def col_peer(j):
        return rem(z + outward(div(j, nk), nz), nz) * nk + rem(k + outward(rem(j, nk), nk), nk)

    def to_rows(fn, sem):
        def one(j, _):
            p = row_peer(j)
            src, dst = fn(p)
            pltpu.make_async_remote_copy(src_ref=src, dst_ref=dst, send_sem=sem.at[0], recv_sem=sem.at[1],
                                         device_id=(p, c), device_id_type=MESH).start()
        for j in range(rows - 1):
            one(j, 0)

    def to_cols(fn, sem):
        def one(j, _):
            p = col_peer(j)
            src, dst = fn(p)
            pltpu.make_async_remote_copy(src_ref=src, dst_ref=dst, send_sem=sem.at[0], recv_sem=sem.at[1],
                                         device_id=(r, p), device_id_type=MESH).start()
        for j in range(cols - 1):
            one(j, 0)

    def settle(ref, sem):
        pltpu.make_async_copy(ref, ref, sem).wait()

    barrier = pltpu.get_barrier_semaphore()

    def greet_row(j, _):
        pl.semaphore_signal(barrier, inc=1, device_id=(row_peer(j), c), device_id_type=MESH)
        return 0

    def greet_col(j, _):
        pl.semaphore_signal(barrier, inc=1, device_id=(r, col_peer(j)), device_id_type=MESH)
        return 0

    lax.fori_loop(0, rows - 1, greet_row, 0)
    lax.fori_loop(0, cols - 1, greet_col, 0)
    loads = [pltpu.make_async_copy(src, dst, in_sem.at[i]) for i, (src, dst) in enumerate((
        (s0_hbm, s0), (win_hbm, small.at[0]), (inp_hbm, inp), (w_hbm, wb), (fb_hbm, small.at[1]), (wo_hbm, wob),
        (tgt_hbm, tgt), (gain_hbm, gain_ref), (decay_hbm, decay_ref)))]
    for load in loads:
        load.start()

    own_rows = pl.ds(pl.multiple_of(r * own, own), own)
    own_k = pl.ds(pl.multiple_of(c * kp, kp), kp)
    below_nb = lax.broadcasted_iota(jnp.int32, (nb, batch), 1) < half

    def turned(array):
        return pltpu.roll(array, half, 1)

    def paired(one, two):
        low = lax.broadcasted_iota(jnp.int32, one.shape, 1) < half
        return jnp.where(low, one, turned(two)), jnp.where(low, turned(one), two)

    def piece(ref):
        return jnp.concatenate([ref[pl.ds(pl.multiple_of(a * nb + c * 8, 8), 8), :] for a in range(groups)], axis=0)

    def packed(full):
        return paired(full[:own], full[own:])

    loads[0].wait()
    for a in range(groups):
        nat[a * nb:(a + 1) * nb, :] = s0[pl.ds(a, batch, stride=groups), :].astype(F32).T
    for p, tile in enumerate(packed(piece(nat))):
        S[0, p, own_rows, :] = tile.astype(BF16)
    pl.semaphore_wait(barrier, rows + cols - 2)
    for p in range(2):
        to_rows(lambda q: (S.at[0, p, own_rows], S.at[0, p, own_rows]), s_sem.at[0, p])

    loads[7].wait()
    loads[8].wait()
    for a in range(groups):
        at = slice(a * nb, (a + 1) * nb)
        gain[at, :] = jnp.broadcast_to(gain_ref[a:a + 1, :], (batch, nb)).T
        decay[at, :] = jnp.broadcast_to(decay_ref[a:a + 1, :], (batch, nb)).T
    g_own, d_own = packed(piece(gain)), packed(piece(decay))
    loads[1].wait()
    smallf[...] = small[0].astype(F32)
    for a in range(groups):
        nat[a * nb:(a + 1) * nb, :] = smallf[pl.ds(a, kn, stride=groups), :].T
    winb[...] = piece(nat).astype(BF16)
    loads[3].wait()
    part = wb.shape[0] // 8
    for i in range(8):
        wf[i * part:(i + 1) * part, :] = wb[i * part:(i + 1) * part, :].astype(F32)
    loads[2].wait()

    def outside(t, _):
        full = lax.dot_general(winb[...], inp[t].astype(F32).astype(BF16), (((1,), (1,)), ((), ())),
                               preferred_element_type=F32)
        one, two = packed(full)
        ext[t, 0], ext[t, 1] = one, two
        return 0

    lax.fori_loop(0, steps, outside, 0)
    for a in range(groups):
        wa = wf[pl.ds(a, ns, stride=groups), :].reshape(rows, 2, own, nb)
        for h in range(2):
            place = h if a < groups // 2 else 1 - h
            wt[a * nb:(a + 1) * nb, place * (ns // 2):(place + 1) * (ns // 2)] = (
                wa[:, h].reshape(ns // 2, nb).T.astype(BF16))
    loads[4].wait()
    smallf[...] = small[1].astype(F32)
    for a in range(groups):
        fbt[a * nb:(a + 1) * nb, :] = smallf[pl.ds(a, kn, stride=groups), :].T.astype(BF16)
    loads[5].wait()
    for a in range(groups):
        wok[:, a * nb:(a + 1) * nb] = wob[a * nb:(a + 1) * nb, :].astype(F32).T
    loads[6].wait()
    v[...] = jnp.zeros_like(v)
    u[...] = jnp.zeros_like(u)
    tr[...] = jnp.zeros_like(tr)
    rd[...] = jnp.zeros_like(rd)

    def drive(t, p):
        settle(S.at[t, p, pl.ds(0, (rows - 1) * own)], s_sem.at[t, p, 1])
        here = S[t, p]
        over = turned(here.astype(F32)).astype(BF16)
        SR[p] = over
        out = jnp.dot(wt[...], jnp.concatenate([here, over], axis=0), preferred_element_type=F32)
        for a in range(groups // 2):
            b = a + groups // 2
            CT[p, a * nb:(a + 1) * nb, :] = jnp.where(
                below_nb, out[a * nb:(a + 1) * nb], out[b * nb:(b + 1) * nb])
        for cc in range(cols):
            CS[t, p, cc] = jnp.concatenate(
                [CT[p, a * nb + cc * 8:a * nb + cc * 8 + 8, :] for a in range(groups // 2)], axis=0).astype(BF16)
        to_cols(lambda q: (CS.at[t, p, q], CR.at[t, p, c]), c_sem.at[t, p])
        CR[t, p, c] = jnp.zeros((own, batch), BF16)

    def move(t, p):
        mine = jnp.concatenate(
            [CT[p, pl.ds(pl.multiple_of(a * nb + c * 8, 8), 8), :] for a in range(groups // 2)], axis=0)
        spike = S[t, p, own_rows, :].astype(F32)
        kept = LEAK * v[p] + (ext[t, p] + mine) - spike
        adapt = d_own[p] * u[p] + spike
        u[p] = adapt
        settle(CR.at[t, p, pl.ds(0, cols - 1)], c_sem.at[t, p, 1])
        volt = kept + jnp.sum(CR[t, p].astype(F32), axis=0)
        v[p] = volt
        rate = jax.nn.sigmoid(volt - 1.0 - g_own[p] * adapt).astype(BF16)

        @pl.when(t + 1 < steps)
        def _():
            S[t + 1, p, own_rows, :] = rate
            to_rows(lambda q: (S.at[t + 1, p, own_rows], S.at[t + 1, p, own_rows]), s_sem.at[t + 1, p])

        F[t, c, p * own:(p + 1) * own, :] = rate

    def spread(t):
        to_cols(lambda q: (F.at[t, c], F.at[t, c]), f_sem.at[t])

    def project(t):
        settle(F.at[t, pl.ds(0, cols - 1)], f_sem.at[t, 1])
        halves = [F[t, :, p * own:(p + 1) * own, :].astype(F32).reshape(cols * own, batch) for p in range(2)]
        natural = []
        for full in paired(*halves):
            full = full.reshape(cols, groups // 2, 8, batch)
            natural += [full[:, a].reshape(nb, batch) for a in range(groups // 2)]
        QS[t] = jnp.dot(wok[own_k, :].astype(BF16), jnp.concatenate(natural, axis=0).astype(BF16),
                        preferred_element_type=F32)
        QR[t, r] = QS[t]
        to_rows(lambda q: (QS.at[t], QR.at[t, r]), q_sem.at[t])
        for a in range(groups):
            SL[t, a * nb:(a + 1) * nb, :] = natural[a] * (1.0 - natural[a])

    def gather(t):
        settle(QR.at[t, pl.ds(0, rows - 1)], q_sem.at[t, 1])
        RO[t, own_k, :] = jnp.sum(QR[t], axis=0)
        to_cols(lambda q: (RO.at[t, own_k], RO.at[t, own_k]), r_sem.at[t])

    def learn(t):
        settle(RO.at[t, pl.ds(0, (cols - 1) * kp)], r_sem.at[t, 1])
        level = READ_DECAY * rd[...] + RO[t]
        rd[...] = level
        err = jax.nn.sigmoid(level) - tgt[t].astype(F32).T
        high = err.astype(BF16)
        low = (err - high.astype(F32)).astype(BF16)
        signal = jnp.dot(fbt[...], high, preferred_element_type=F32) + jnp.dot(fbt[...], low, preferred_element_type=F32)
        WG[t] = signal * SL[t]
        levels[t] = level.T

    def trace(t):
        for h, full in enumerate((jnp.where(below_ns, S[t, 0].astype(F32), SR[1].astype(F32)),
                                  jnp.where(below_ns, SR[0].astype(F32), S[t, 1].astype(F32)))):
            now = LEAK * tr[h] + full
            tr[h] = now
            TR[t, :, h] = now.astype(BF16).reshape(rows, own, batch)

    below_ns = lax.broadcasted_iota(jnp.int32, (ns // 2, batch), 1) < half

    def step(t, _):
        drive(t, 0)
        drive(t, 1)
        trace(t)

        @pl.when(t >= 2)
        def _():
            gather(t - 2)

        move(t, 0)
        move(t, 1)
        spread(t)

        @pl.when(t >= 1)
        def _():
            project(t - 1)

        @pl.when(t >= 3)
        def _():
            learn(t - 3)
        return 0

    lax.fori_loop(0, steps, step, 0)
    last = steps - 1
    gather(last - 1)
    learn(last - 2)
    project(last)
    learn(last - 1)
    gather(last)
    learn(last)

    chunk = min(64, nr)

    def back(i, _):
        at = pl.ds(pl.multiple_of(i * chunk, chunk), chunk)
        g, d = gain[at, :], decay[at, :]
        future = jnp.zeros((chunk, batch), F32)
        for t in reversed(range(steps)):
            w, sl = WG[t, at, :], SL[t, at, :]
            gs = g * sl
            FT[t, at, :] = (w - gs * future).astype(BF16)
            future = w + (d - gs) * future
        return 0

    lax.fori_loop(0, nr // chunk, back, 0)

    block = min(8, rows)
    sq[...] = jnp.zeros_like(sq)

    def grads(i, _):
        at = pl.ds(i * block, block)
        count = block * 2 * own
        lhs = jnp.concatenate([TR[t, at].reshape(count, batch) for t in range(steps)], axis=1)
        rhs = jnp.concatenate([FT[t] for t in range(steps)], axis=1)
        out = lax.dot_general(lhs, rhs, (((1,), (1,)), ((), ())), preferred_element_type=F32)
        for a in range(groups):
            grad[pl.ds(i * (count * groups) + a, count, stride=groups), :] = out[:, a * nb:(a + 1) * nb]
        store = pl.ds(pl.multiple_of(i * (count * groups), count * groups), count * groups)
        pltpu.make_async_copy(grad.at[store], grad_hbm.at[store], out_sem.at[0]).start()
        two = jnp.sum((out * out).reshape(count // 8, 8, nr), axis=0)
        sq[...] += sum(two[:, i * nb:(i + 1) * nb] for i in range(groups))
        return 0

    pltpu.make_async_copy(levels, levels_hbm, out_sem.at[1]).start()
    lax.fori_loop(0, rows // block, grads, 0)
    N1[r] = sq[...]
    to_rows(lambda p: (sq, N1.at[r]), n_sem.at[0])
    settle(N1.at[pl.ds(0, rows - 1)], n_sem.at[0, 1])
    settle(N1.at[pl.ds(0, rows - 1)], n_sem.at[0, 0])
    sq[...] = jnp.sum(N1[...], axis=0)
    N2[c] = sq[...]
    to_cols(lambda p: (sq, N2.at[c]), n_sem.at[1])

    def ends(t, _):
        for p in range(2):
            settle(S.at[t, p, pl.ds(0, (rows - 1) * own)], s_sem.at[t, p, 0])
            settle(CR.at[t, p, pl.ds(0, cols - 1)], c_sem.at[t, p, 0])
        settle(F.at[t, pl.ds(0, cols - 1)], f_sem.at[t, 0])
        settle(QR.at[t, pl.ds(0, rows - 1)], q_sem.at[t, 0])
        settle(RO.at[t, pl.ds(0, (cols - 1) * kp)], r_sem.at[t, 0])
        return 0

    lax.fori_loop(0, steps, ends, 0)
    settle(N2.at[pl.ds(0, cols - 1)], n_sem.at[1, 1])
    settle(N2.at[pl.ds(0, cols - 1)], n_sem.at[1, 0])
    total = jnp.sum(jnp.sum(N2[...], axis=0), keepdims=True)
    factor = jnp.minimum(1.0, neurons / 16.0 / jnp.sqrt(total + 1e-06))
    clip[...] = jnp.broadcast_to(factor, clip.shape)
    pltpu.make_async_copy(clip, clip_hbm, out_sem.at[2]).start()
    settle(grad, out_sem.at[0])
    settle(levels, out_sem.at[1])
    settle(clip, out_sem.at[2])


def finish(levels_hbm, grad_hbm, clip_hbm, readout_hbm, scaled_hbm, grad, levels, clip, sem):
    parts = 4
    part = grad.shape[0] // parts
    at = [pl.ds(i * part, part) for i in range(parts)]
    bring = pltpu.make_async_copy(levels_hbm, levels, sem.at[2 * parts])
    last = pltpu.make_async_copy(levels, readout_hbm, sem.at[2 * parts + 2])
    factor = pltpu.make_async_copy(clip_hbm, clip, sem.at[2 * parts + 1])
    loads = [pltpu.make_async_copy(grad_hbm.at[at[i]], grad.at[at[i]], sem.at[i]) for i in range(parts)]
    stores = [pltpu.make_async_copy(grad.at[at[i]], scaled_hbm.at[at[i]], sem.at[parts + i]) for i in range(parts)]
    factor.start()
    for load in loads:
        load.start()
    bring.start()
    factor.wait()
    for i in range(parts):
        loads[i].wait()
        grad[at[i], :] = grad[at[i], :] * clip[0:1, :]
        stores[i].start()
    bring.wait()
    last.start()
    for store in stores:
        store.wait()
    last.wait()


def body(dims, inputs, targets, initial_spikes, w_in, w_rec, w_out, feedback, adapt_gain, adapt_decay):
    ny, nx, nz, nk, nb, steps, neurons = dims
    rows, cols = ny * nx, nz * nk
    batch, channels = inputs.shape[1:]
    own_cols, groups = w_rec.shape[1], w_rec.shape[2]
    own = groups * own_cols // 2
    ns, nr = w_rec.shape[0] * own_cols, groups * nb
    kn = w_out.shape[2]
    kp = kn // cols
    dma = pltpu.SemaphoreType.DMA
    V = pltpu.VMEM
    far = pl.BlockSpec(memory_space=pltpu.HBM)
    grad, levels, clip = pl.pallas_call(
        functools.partial(kernel, dims),
        out_shape=(
            jax.ShapeDtypeStruct((ns * groups, nb), F32),
            jax.ShapeDtypeStruct((steps, batch, kn), F32),
            jax.ShapeDtypeStruct((8, nb), F32),
        ),
        in_specs=[far] * 9,
        out_specs=(far, far, far),
        scratch_shapes=[
            V((ns * groups, nb), F32),
            V((steps, batch, kn), F32),
            V((8, nb), F32),
            V((ns * groups, nb), BF16),
            V((ns * groups, nb), F32),
            V((nr, ns), BF16),
            V((steps, batch, channels), jnp.int32),
            V((steps, batch, kn), jnp.int32),
            V((batch * groups, nb), jnp.int32),
            V((2, kn * groups, nb), BF16),
            V((nr, kn), BF16),
            V((kn * groups, nb), F32),
            V((groups, nb), F32),
            V((groups, nb), F32),
            V((nr, batch), F32),
            V((nr, kn), BF16),
            V((2 * own, channels), BF16),
            V((kn, nr), F32),
            V((nr, batch), F32),
            V((nr, batch), F32),
            V((steps, 2, own, batch), F32),
            V((steps, 2, rows * own, batch), BF16),
            V((2, rows * own, batch), BF16),
            V((steps, cols, 2 * own, batch), BF16),
            V((steps, 2, cols, own, batch), BF16),
            V((steps, 2, cols, own, batch), BF16),
            V((2, nr // 2, batch), F32),
            V((2, own, batch), F32),
            V((2, own, batch), F32),
            V((steps, kp, batch), F32),
            V((steps, rows, kp, batch), F32),
            V((steps, kn, batch), F32),
            V((kn, batch), F32),
            V((steps, rows, 2, own, batch), BF16),
            V((2, rows * own, batch), F32),
            V((steps, nr, batch), F32),
            V((steps, nr, batch), F32),
            V((steps, nr, batch), BF16),
            V((8, nb), F32),
            V((rows, 8, nb), F32),
            V((cols, 8, nb), F32),
            dma((9,)), dma((steps, 2, 2)), dma((steps, 2)), dma((steps, 2, 2)), dma((steps, 2)), dma((steps, 2)),
            dma((2, 2)), dma((3,)),
        ],
        compiler_params=pltpu.CompilerParams(
            collective_id=0, has_side_effects=True, vmem_limit_bytes=63 * 2**20
        ),
    )(w_rec.reshape(ns * groups, nb), inputs, targets, initial_spikes.reshape(batch * groups, nb),
      w_in.reshape(channels * groups, nb), w_out.reshape(nr, kn), feedback.reshape(kn * groups, nb), adapt_gain, adapt_decay)
    readout, scaled = pl.pallas_call(
        finish,
        out_shape=(
            jax.ShapeDtypeStruct((steps, batch, kn), F32),
            jax.ShapeDtypeStruct((ns * groups, nb), F32),
        ),
        in_specs=[far] * 3,
        out_specs=(far, far),
        scratch_shapes=[V((ns * groups, nb), F32), V((steps, batch, kn), F32), V((8, nb), F32), dma((11,))],
        compiler_params=pltpu.CompilerParams(vmem_limit_bytes=63 * 2**20),
    )(levels, grad, clip)
    return readout, scaled.reshape(w_rec.shape)


def build(mesh, split, na, nb, steps):
    dims = (*split, nb, steps, na * nb)
    placed = (
        P(),
        P(),
        P(None, "row", None),
        P(None, "row", None),
        P(None, "col", "row", None),
        P("row", None, None),
        P(None, "row", None),
        P("row", None),
        P("row", None),
    )
    return jax.shard_map(
        functools.partial(body, dims), mesh=mesh, in_specs=placed,
        out_specs=(P(), P(None, "col", "row", None)), check_vma=False,
    )


def solution(mesh):
    return build(mesh, (8, 4, 8, 2), 128, 128, 8)
```

```python
import functools

import jax
import jax.numpy as jnp
from jax import lax
from jax.experimental import pallas as pl
from jax.experimental.pallas import tpu as pltpu
from jax.sharding import PartitionSpec as P

MESH = pl.DeviceIdType.MESH
LEAK = 0.8
READ_DECAY = 0.8
F32 = jnp.float32
BF16 = jnp.bfloat16


def rem(a, b):
    return a % b if isinstance(a, int) else lax.rem(a, jnp.int32(b))


def div(a, b):
    return a // b if isinstance(a, int) else lax.div(a, jnp.int32(b))


def outward(i, n):
    return n // 2 + (1 - 2 * rem(i, 2)) * div(i + 1, 2)


def kernel(dims, w_hbm, inp_hbm, tgt_hbm, s0_hbm, win_hbm, wo_hbm, fb_hbm, gain_hbm, decay_hbm, grad_hbm, levels_hbm, clip_hbm,
           grad, levels, clip,
           wb, wf, wt, inp, tgt, s0, small, wob, smallf, gain_ref, decay_ref, nat, fbt, winb, wok, gain, decay, ext,
           S, SR, F, CS, CR, CT, v, u, QS, QR, RO, rd, TR, tr, SL, WG, FT, sq, one, two, N1, N2,
           in_sem, s_sem, f_sem, c_sem, q_sem, r_sem, n_sem, out_sem):
    ny, nx, nz, nk, nb, steps, neurons = dims
    rows, cols = ny * nx, nz * nk
    r, c = lax.axis_index("row"), lax.axis_index("col")
    y, x, z, k = div(r, nx), rem(r, nx), div(c, nk), rem(c, nk)
    batch = inp.shape[1]
    half = batch // 2
    nr, ns = wt.shape
    kn = tgt.shape[2]
    kp = kn // cols
    groups = nr // nb
    own = groups * 8 // 2

    def row_peer(j):
        return rem(y + outward(div(j, nx), ny), ny) * nx + rem(x + outward(rem(j, nx), nx), nx)

    def col_peer(j):
        return rem(z + outward(div(j, nk), nz), nz) * nk + rem(k + outward(rem(j, nk), nk), nk)

    def to_rows(fn, sem):
        def one(j, _):
            p = row_peer(j)
            src, dst = fn(p)
            pltpu.make_async_remote_copy(src_ref=src, dst_ref=dst, send_sem=sem.at[0], recv_sem=sem.at[1],
                                         device_id=(p, c), device_id_type=MESH).start()
        for j in range(rows - 1):
            one(j, 0)

    def to_cols(fn, sem):
        def one(j, _):
            p = col_peer(j)
            src, dst = fn(p)
            pltpu.make_async_remote_copy(src_ref=src, dst_ref=dst, send_sem=sem.at[0], recv_sem=sem.at[1],
                                         device_id=(r, p), device_id_type=MESH).start()
        for j in range(cols - 1):
            one(j, 0)

    def settle(ref, sem):
        pltpu.make_async_copy(ref, ref, sem).wait()

    barrier = pltpu.get_barrier_semaphore()

    def greet_row(j, _):
        pl.semaphore_signal(barrier, inc=1, device_id=(row_peer(j), c), device_id_type=MESH)
        return 0

    def greet_col(j, _):
        pl.semaphore_signal(barrier, inc=1, device_id=(r, col_peer(j)), device_id_type=MESH)
        return 0

    lax.fori_loop(0, rows - 1, greet_row, 0)
    lax.fori_loop(0, cols - 1, greet_col, 0)
    loads = [pltpu.make_async_copy(src, dst, in_sem.at[i]) for i, (src, dst) in enumerate((
        (s0_hbm, s0), (win_hbm, small.at[0]), (inp_hbm, inp), (w_hbm, wb), (fb_hbm, small.at[1]), (wo_hbm, wob),
        (tgt_hbm, tgt), (gain_hbm, gain_ref), (decay_hbm, decay_ref)))]
    for load in loads:
        load.start()

    own_rows = pl.ds(pl.multiple_of(r * own, own), own)
    own_k = pl.ds(pl.multiple_of(c * kp, kp), kp)
    below_nb = lax.broadcasted_iota(jnp.int32, (nb, batch), 1) < half

    def turned(array):
        return pltpu.roll(array, half, 1)

    def paired(one, two):
        low = lax.broadcasted_iota(jnp.int32, one.shape, 1) < half
        return jnp.where(low, one, turned(two)), jnp.where(low, turned(one), two)

    def piece(ref):
        return jnp.concatenate([ref[pl.ds(pl.multiple_of(a * nb + c * 8, 8), 8), :] for a in range(groups)], axis=0)

    def packed(full):
        return paired(full[:own], full[own:])

    loads[0].wait()
    for a in range(groups):
        nat[a * nb:(a + 1) * nb, :] = s0[pl.ds(a, batch, stride=groups), :].astype(F32).T
    for p, tile in enumerate(packed(piece(nat))):
        S[0, p, own_rows, :] = tile.astype(BF16)
    pl.semaphore_wait(barrier, rows + cols - 2)
    for p in range(2):
        to_rows(lambda q: (S.at[0, p, own_rows], S.at[0, p, own_rows]), s_sem.at[0, p])

    loads[7].wait()
    loads[8].wait()
    for a in range(groups):
        at = slice(a * nb, (a + 1) * nb)
        gain[at, :] = jnp.broadcast_to(gain_ref[a:a + 1, :], (batch, nb)).T
        decay[at, :] = jnp.broadcast_to(decay_ref[a:a + 1, :], (batch, nb)).T
    g_own, d_own = packed(piece(gain)), packed(piece(decay))
    loads[1].wait()
    smallf[...] = small[0].astype(F32)
    for a in range(groups):
        nat[a * nb:(a + 1) * nb, :] = smallf[pl.ds(a, kn, stride=groups), :].T
    winb[...] = piece(nat).astype(BF16)
    loads[3].wait()
    part = wb.shape[0] // 8
    for i in range(8):
        wf[i * part:(i + 1) * part, :] = wb[i * part:(i + 1) * part, :].astype(F32)
    loads[2].wait()

    def outside(t, _):
        full = lax.dot_general(winb[...], inp[t].astype(F32).astype(BF16), (((1,), (1,)), ((), ())),
                               preferred_element_type=F32)
        ext[t, 0], ext[t, 1] = packed(full)
        return 0

    lax.fori_loop(0, steps, outside, 0)
    for a in range(groups):
        wa = wf[pl.ds(a, ns, stride=groups), :].reshape(rows, 2, own, nb)
        for h in range(2):
            place = h if a < groups // 2 else 1 - h
            wt[a * nb:(a + 1) * nb, place * (ns // 2):(place + 1) * (ns // 2)] = (
                wa[:, h].reshape(ns // 2, nb).T.astype(BF16))
    loads[4].wait()
    smallf[...] = small[1].astype(F32)
    for a in range(groups):
        fbt[a * nb:(a + 1) * nb, :] = smallf[pl.ds(a, kn, stride=groups), :].T.astype(BF16)
    loads[5].wait()
    for a in range(groups):
        wok[:, a * nb:(a + 1) * nb] = wob[a * nb:(a + 1) * nb, :].astype(F32).T
    loads[6].wait()
    v[...] = jnp.zeros_like(v)
    u[...] = jnp.zeros_like(u)
    tr[...] = jnp.zeros_like(tr)
    rd[...] = jnp.zeros_like(rd)

    def drive(t, p):
        settle(S.at[t, p, pl.ds(0, (rows - 1) * own)], s_sem.at[t, p, 1])
        here = S[t, p]
        over = jnp.concatenate([here[:, half:], here[:, :half]], axis=1)
        SR[p] = over
        out = jnp.dot(wt[...], jnp.concatenate([here, over], axis=0), preferred_element_type=F32)
        for a in range(groups // 2):
            b = a + groups // 2
            CT[p, a * nb:(a + 1) * nb, :] = jnp.where(
                below_nb, out[a * nb:(a + 1) * nb], out[b * nb:(b + 1) * nb])
        for cc in range(cols):
            CS[t, p, cc] = jnp.concatenate(
                [CT[p, a * nb + cc * 8:a * nb + cc * 8 + 8, :] for a in range(groups // 2)], axis=0).astype(BF16)
        to_cols(lambda q: (CS.at[t, p, q], CR.at[t, p, c]), c_sem.at[t, p])
        CR[t, p, c] = jnp.zeros((own, batch), BF16)

    def move(t, p):
        mine = jnp.concatenate(
            [CT[p, pl.ds(pl.multiple_of(a * nb + c * 8, 8), 8), :] for a in range(groups // 2)], axis=0)
        spike = S[t, p, own_rows, :].astype(F32)
        kept = LEAK * v[p] + (ext[t, p] + mine) - spike
        adapt = d_own[p] * u[p] + spike
        u[p] = adapt
        settle(CR.at[t, p, pl.ds(0, cols - 1)], c_sem.at[t, p, 1])
        volt = kept + jnp.sum(CR[t, p].astype(F32), axis=0)
        v[p] = volt
        rate = jax.nn.sigmoid(volt - 1.0 - g_own[p] * adapt).astype(BF16)

        @pl.when(t + 1 < steps)
        def _():
            S[t + 1, p, own_rows, :] = rate
            to_rows(lambda q: (S.at[t + 1, p, own_rows], S.at[t + 1, p, own_rows]), s_sem.at[t + 1, p])

        mine = pl.ds(p * own, own)
        F[t, c, mine, :] = rate

        @pl.when(t + 1 == steps)
        def _():
            to_cols(lambda q: (F.at[t, c, mine], F.at[t, c, mine]), f_sem.at[t])

    def spread(t):
        to_cols(lambda q: (F.at[t, c], F.at[t, c]), f_sem.at[t])

    def project(t):
        settle(F.at[t, pl.ds(0, cols - 1)], f_sem.at[t, 1])
        halves = [F[t, :, p * own:(p + 1) * own, :].astype(F32).reshape(cols * own, batch) for p in range(2)]
        natural = []
        for full in paired(*halves):
            full = full.reshape(cols, groups // 2, 8, batch)
            natural += [full[:, a].reshape(nb, batch) for a in range(groups // 2)]
        QS[t] = jnp.dot(wok[own_k, :].astype(BF16), jnp.concatenate(natural, axis=0).astype(BF16),
                        preferred_element_type=F32)
        QR[t, r] = QS[t]
        to_rows(lambda q: (QS.at[t], QR.at[t, r]), q_sem.at[t])
        for a in range(groups):
            SL[t, a * nb:(a + 1) * nb, :] = natural[a] * (1.0 - natural[a])

    def gather(t):
        settle(QR.at[t, pl.ds(0, rows - 1)], q_sem.at[t, 1])
        RO[t, own_k, :] = jnp.sum(QR[t], axis=0)
        to_cols(lambda q: (RO.at[t, own_k], RO.at[t, own_k]), r_sem.at[t])

    def learn(t):
        settle(RO.at[t, pl.ds(0, (cols - 1) * kp)], r_sem.at[t, 1])
        level = READ_DECAY * rd[...] + RO[t]
        rd[...] = level
        err = jax.nn.sigmoid(level) - tgt[t].astype(F32).T
        high = err.astype(BF16)
        low = (err - high.astype(F32)).astype(BF16)
        signal = jnp.dot(fbt[...], high, preferred_element_type=F32) + jnp.dot(fbt[...], low, preferred_element_type=F32)
        WG[t] = signal * SL[t]
        levels[t] = level.T

    def trace(t):
        for h, full in enumerate((jnp.where(below_ns, S[t, 0].astype(F32), SR[1].astype(F32)),
                                  jnp.where(below_ns, SR[0].astype(F32), S[t, 1].astype(F32)))):
            now = LEAK * tr[h] + full
            tr[h] = now
            TR[t, :, h] = now.astype(BF16).reshape(rows, own, batch)

    below_ns = lax.broadcasted_iota(jnp.int32, (ns // 2, batch), 1) < half

    last = steps - 1

    def step(t, _):
        drive(t, 0)
        drive(t, 1)

        @pl.when(t >= 1)
        def _():
            project(t - 1)

        trace(t)
        move(t, 0)
        move(t, 1)

        @pl.when(t < last)
        def _():
            spread(t)

        @pl.when(t >= 2)
        def _():
            learn(t - 2)

        @pl.when(t >= 1)
        def _():
            gather(t - 1)
        return 0

    lax.fori_loop(0, steps, step, 0)
    project(last)
    learn(last - 1)
    gather(last)
    learn(last)

    chunk = min(64, nr)

    def back(i, _):
        at = pl.ds(pl.multiple_of(i * chunk, chunk), chunk)
        g, d = gain[at, :], decay[at, :]
        future = jnp.zeros((chunk, batch), F32)
        for t in reversed(range(steps)):
            w, sl = WG[t, at, :], SL[t, at, :]
            gs = g * sl
            FT[t, at, :] = (w - gs * future).astype(BF16)
            future = w + (d - gs) * future
        return 0

    lax.fori_loop(0, nr // chunk, back, 0)

    block = min(8, rows)
    sq[...] = jnp.zeros_like(sq)

    def grads(i, _):
        at = pl.ds(i * block, block)
        count = block * 2 * own
        lhs = jnp.concatenate([TR[t, at].reshape(count, batch) for t in range(steps)], axis=1)
        rhs = jnp.concatenate([FT[t] for t in range(steps)], axis=1)
        out = lax.dot_general(lhs, rhs, (((1,), (1,)), ((), ())), preferred_element_type=F32)
        for a in range(groups):
            grad[pl.ds(i * (count * groups) + a, count, stride=groups), :] = out[:, a * nb:(a + 1) * nb]
        store = pl.ds(pl.multiple_of(i * (count * groups), count * groups), count * groups)
        pltpu.make_async_copy(grad.at[store], grad_hbm.at[store], out_sem.at[0]).start()
        squares = jnp.sum((out * out).reshape(count // 8, 8, nr), axis=0)
        sq[...] += sum(squares[:, a * nb:(a + 1) * nb] for a in range(groups))
        return 0

    pltpu.make_async_copy(levels, levels_hbm, out_sem.at[1]).start()
    lax.fori_loop(0, rows // block, grads, 0)
    one[...] = jnp.sum(sq[...], axis=0, keepdims=True)
    N1[r] = one[...]
    to_rows(lambda p: (one, N1.at[r]), n_sem.at[0])
    settle(N1.at[pl.ds(0, rows - 1)], n_sem.at[0, 1])
    two[...] = jnp.sum(N1[...], axis=0)
    N2[c] = two[...]
    to_cols(lambda p: (two, N2.at[c]), n_sem.at[1])
    settle(N1.at[pl.ds(0, rows - 1)], n_sem.at[0, 0])

    def ends(t, _):
        for p in range(2):
            settle(S.at[t, p, pl.ds(0, (rows - 1) * own)], s_sem.at[t, p, 0])
            settle(CR.at[t, p, pl.ds(0, cols - 1)], c_sem.at[t, p, 0])
        settle(F.at[t, pl.ds(0, cols - 1)], f_sem.at[t, 0])
        settle(QR.at[t, pl.ds(0, rows - 1)], q_sem.at[t, 0])
        settle(RO.at[t, pl.ds(0, (cols - 1) * kp)], r_sem.at[t, 0])
        return 0

    lax.fori_loop(0, steps, ends, 0)
    settle(N2.at[pl.ds(0, cols - 1)], n_sem.at[1, 1])
    settle(N2.at[pl.ds(0, cols - 1)], n_sem.at[1, 0])
    total = jnp.sum(jnp.sum(N2[...], axis=0), keepdims=True)
    factor = jnp.minimum(1.0, neurons / 16.0 / jnp.sqrt(total + 1e-06))
    clip[...] = jnp.broadcast_to(factor, clip.shape)
    pltpu.make_async_copy(clip, clip_hbm, out_sem.at[2]).start()
    settle(grad, out_sem.at[0])
    settle(levels, out_sem.at[1])
    settle(clip, out_sem.at[2])


def finish(levels_hbm, grad_hbm, clip_hbm, readout_hbm, scaled_hbm, grad, levels, clip, sem):
    parts = 4
    part = grad.shape[0] // parts
    at = [pl.ds(i * part, part) for i in range(parts)]
    bring = pltpu.make_async_copy(levels_hbm, levels, sem.at[2 * parts])
    last = pltpu.make_async_copy(levels, readout_hbm, sem.at[2 * parts + 2])
    factor = pltpu.make_async_copy(clip_hbm, clip, sem.at[2 * parts + 1])
    loads = [pltpu.make_async_copy(grad_hbm.at[at[i]], grad.at[at[i]], sem.at[i]) for i in range(parts)]
    stores = [pltpu.make_async_copy(grad.at[at[i]], scaled_hbm.at[at[i]], sem.at[parts + i]) for i in range(parts)]
    factor.start()
    for load in loads:
        load.start()
    bring.start()
    factor.wait()
    for i in range(parts):
        loads[i].wait()
        grad[at[i], :] = grad[at[i], :] * clip[0:1, :]
        stores[i].start()
    bring.wait()
    last.start()
    for store in stores:
        store.wait()
    last.wait()


def body(dims, inputs, targets, initial_spikes, w_in, w_rec, w_out, feedback, adapt_gain, adapt_decay):
    ny, nx, nz, nk, nb, steps, neurons = dims
    rows, cols = ny * nx, nz * nk
    batch, channels = inputs.shape[1:]
    own_cols, groups = w_rec.shape[1], w_rec.shape[2]
    own = groups * own_cols // 2
    ns, nr = w_rec.shape[0] * own_cols, groups * nb
    kn = w_out.shape[2]
    kp = kn // cols
    dma = pltpu.SemaphoreType.DMA
    V = pltpu.VMEM
    far = pl.BlockSpec(memory_space=pltpu.HBM)
    grad, levels, clip = pl.pallas_call(
        functools.partial(kernel, dims),
        out_shape=(
            jax.ShapeDtypeStruct((ns * groups, nb), F32),
            jax.ShapeDtypeStruct((steps, batch, kn), F32),
            jax.ShapeDtypeStruct((8, nb), F32),
        ),
        in_specs=[far] * 9,
        out_specs=(far, far, far),
        scratch_shapes=[
            V((ns * groups, nb), F32),
            V((steps, batch, kn), F32),
            V((8, nb), F32),
            V((ns * groups, nb), BF16),
            V((ns * groups, nb), F32),
            V((nr, ns), BF16),
            V((steps, batch, channels), jnp.int32),
            V((steps, batch, kn), jnp.int32),
            V((batch * groups, nb), jnp.int32),
            V((2, kn * groups, nb), BF16),
            V((nr, kn), BF16),
            V((kn * groups, nb), F32),
            V((groups, nb), F32),
            V((groups, nb), F32),
            V((nr, batch), F32),
            V((nr, kn), BF16),
            V((2 * own, channels), BF16),
            V((kn, nr), F32),
            V((nr, batch), F32),
            V((nr, batch), F32),
            V((steps, 2, own, batch), F32),
            V((steps, 2, rows * own, batch), BF16),
            V((2, rows * own, batch), BF16),
            V((steps, cols, 2 * own, batch), BF16),
            V((steps, 2, cols, own, batch), BF16),
            V((steps, 2, cols, own, batch), BF16),
            V((2, nr // 2, batch), F32),
            V((2, own, batch), F32),
            V((2, own, batch), F32),
            V((steps, kp, batch), F32),
            V((steps, rows, kp, batch), F32),
            V((steps, kn, batch), F32),
            V((kn, batch), F32),
            V((steps, rows, 2, own, batch), BF16),
            V((2, rows * own, batch), F32),
            V((steps, nr, batch), F32),
            V((steps, nr, batch), F32),
            V((steps, nr, batch), BF16),
            V((8, nb), F32),
            V((1, nb), F32),
            V((1, nb), F32),
            V((rows, 1, nb), F32),
            V((cols, 1, nb), F32),
            dma((9,)), dma((steps, 2, 2)), dma((steps, 2)), dma((steps, 2, 2)), dma((steps, 2)), dma((steps, 2)),
            dma((2, 2)), dma((3,)),
        ],
        compiler_params=pltpu.CompilerParams(
            collective_id=0, has_side_effects=True, vmem_limit_bytes=63 * 2**20
        ),
    )(w_rec.reshape(ns * groups, nb), inputs, targets, initial_spikes.reshape(batch * groups, nb),
      w_in.reshape(channels * groups, nb), w_out.reshape(nr, kn), feedback.reshape(kn * groups, nb), adapt_gain, adapt_decay)
    readout, scaled = pl.pallas_call(
        finish,
        out_shape=(
            jax.ShapeDtypeStruct((steps, batch, kn), F32),
            jax.ShapeDtypeStruct((ns * groups, nb), F32),
        ),
        in_specs=[far] * 3,
        out_specs=(far, far),
        scratch_shapes=[V((ns * groups, nb), F32), V((steps, batch, kn), F32), V((8, nb), F32), dma((11,))],
        compiler_params=pltpu.CompilerParams(vmem_limit_bytes=63 * 2**20),
    )(levels, grad, clip)
    return readout, scaled.reshape(w_rec.shape)


def build(mesh, split, na, nb, steps):
    dims = (*split, nb, steps, na * nb)
    placed = (
        P(),
        P(),
        P(None, "row", None),
        P(None, "row", None),
        P(None, "col", "row", None),
        P("row", None, None),
        P(None, "row", None),
        P("row", None),
        P("row", None),
    )
    return jax.shard_map(
        functools.partial(body, dims), mesh=mesh, in_specs=placed,
        out_specs=(P(), P(None, "col", "row", None)), check_vma=False,
    )


def solution(mesh):
    return build(mesh, (8, 4, 8, 2), 128, 128, 8)
```
